32 devices in a mesh: sx: 4 (over x, core), sy: 8 (over z, y).
Axes of the slice: x: 2, y: 2, z: 4, core: 2. Of those that a mesh axis runs over, the one named last changes fastest.
Arguments:
- loadings: bfloat16 [64, 16, 1024], P(None, 'sx', 'sy'), may hold values from 0.099609375 to 1
- gene_factors: bfloat16 [96, 64, 128], P('sy'), may hold values from 0.019897461 to 0.19921875
- counts: bfloat16 [4, 8, 32, 128, 512], P('sx', 'sy'), may hold values from 0 to 6
- block_ids: int32 [4, 8, 32], P('sx', 'sy'), may hold values from 0 to 95, as said below
- live: int32 [4, 8], P('sx', 'sy'), may hold values from 1 to 32, as said below
Outputs:
- grad_loadings: float32 [64, 16, 1024], P(None, 'sx', 'sy')
- grad_genes: float32 [96, 64, 128], P('sy')
The draws below stay inside these ranges and needn't reach their ends.
Inputs may be any that keep to these rules, and one draw needn't show every extreme that they name: `block_ids`: the 32 entries of one tile are different gene blocks; slots from live onward are ignored. `live`: some tile uses all 32 slots.
All inputs are finite; a program needn't handle non-finite values.
Results may differ from the reference program's by a relative error of at most 0.0003.
Values may be sent and summed in bfloat16 or wider, within the bound.
A program may use at most 64 MiB of HBM per device.

```python
import math
import jax
import jax.numpy as jnp
from jax import lax

K = 64
GB = 128
NGB = 96
BLK = 32
SP = 512
NR = 16
NC = 1024
N_SX = 4
N_SY = 8


def draw_block_ids(key, part):
    keys = jax.random.split(jax.random.fold_in(key, 11), N_SX * N_SY)
    perms = jax.vmap(lambda k: jax.random.permutation(k, NGB))(keys)
    return perms[:, :BLK].reshape(N_SX, N_SY, BLK).astype(jnp.int32)


def draw_live(key, part):
    counts_key = jax.random.fold_in(key, 23)
    pick_key = jax.random.fold_in(key, 29)
    flat = jax.random.randint(counts_key, (N_SX * N_SY,), 1, BLK + 1)
    spot = jax.random.randint(pick_key, (), 0, N_SX * N_SY)
    flat = flat.at[spot].set(BLK)
    return flat.reshape(N_SX, N_SY).astype(jnp.int32)


def shard_levels(own_key, dims, pieces, low, high):
    factor_of, own = 1.0, jax.random.fold_in(own_key, 6)
    for axis_at, shards_of in pieces:
        draws = jnp.exp(jax.random.uniform(jax.random.fold_in(own, axis_at), (shards_of,), jnp.float32, low / len(pieces), high / len(pieces)))
        factor_of = factor_of * jnp.repeat(draws, dims[axis_at] // shards_of).reshape([-1 if axis == axis_at else 1 for axis in range(len(dims))])
    return factor_of


def setup_inputs(seed: int = 0) -> dict:
    key_of = jax.random.split(jax.random.key(seed), 6)
    loadings = jnp.clip(jnp.exp(math.log(1.0) - 2.306499 * jax.random.uniform(key_of[0], (K, NR, NC), jnp.float32) ** shard_levels(key_of[0], (K, NR, NC), ((1, 4), (2, 8)), -0.2, 0.2)), 0.099609375, 1.0).astype(jnp.bfloat16)
    gene_factors = jnp.clip(jnp.exp(math.log(0.19921875) - 2.3038113 * jax.random.uniform(key_of[1], (NGB, K, GB), jnp.float32) ** shard_levels(key_of[1], (NGB, K, GB), ((0, 8),), -0.2, 0.2)), 0.019897461, 0.19921875).astype(jnp.bfloat16)
    counts = jnp.clip(6.0 * jax.random.uniform(key_of[2], (N_SX, N_SY, BLK, GB, SP), jnp.float32) ** shard_levels(key_of[2], (N_SX, N_SY, BLK, GB, SP), ((0, 4), (1, 8)), -0.2, 0.2), 0.0, 6.0).astype(jnp.bfloat16)
    block_ids = draw_block_ids(jax.random.fold_in(key_of[5], 71), 0)
    live = draw_live(jax.random.fold_in(key_of[5], 71), 0)
    return {"loadings": loadings, "gene_factors": gene_factors, "counts": counts, "block_ids": block_ids, "live": live}


def tile_terms(wflat, factors, tile_counts, tile_ids, tile_live, dense):
    def step(n, carry):
        grad_part, dense_acc = carry
        block = tile_ids[n]
        block_factor = lax.dynamic_index_in_dim(factors, block, 0, keepdims=False)
        block_counts = lax.dynamic_index_in_dim(tile_counts, n, 0, keepdims=False)
        rate = lax.dot_general(block_factor, wflat, (((0,), (0,)), ((), ())), preferred_element_type=jnp.float32)
        ratio = (1.0 - block_counts.astype(jnp.float32) / rate).astype(jnp.bfloat16)
        grad_part = grad_part + lax.dot_general(block_factor, ratio, (((1,), (0,)), ((), ())), preferred_element_type=jnp.float32)
        gene_term = lax.dot_general(wflat, ratio, (((1,), (1,)), ((), ())), preferred_element_type=jnp.float32)
        old = lax.dynamic_index_in_dim(dense_acc, block, 0, keepdims=True)
        dense_acc = lax.dynamic_update_index_in_dim(dense_acc, old + gene_term[None], block, 0)
        return grad_part, dense_acc
    start = jnp.zeros((wflat.shape[0], wflat.shape[1]), jnp.float32)
    return lax.fori_loop(0, tile_live, step, (start, dense))


def reference(loadings, gene_factors, counts, block_ids, live):
    tiles_x = counts.shape[0]
    tiles_y = counts.shape[1]
    rows = loadings.shape[1] // tiles_x
    cols = loadings.shape[2] // tiles_y
    nfac = loadings.shape[0]

    def per_tile(t, carry):
        grad_all, dense = carry
        ti = t // tiles_y
        tj = t % tiles_y
        w_tile = lax.dynamic_slice(loadings, (jnp.int32(0), (ti * rows).astype(jnp.int32), (tj * cols).astype(jnp.int32)), (nfac, rows, cols))
        wflat = w_tile.reshape(nfac, rows * cols)
        part, dense = tile_terms(wflat, gene_factors, counts[ti, tj], block_ids[ti, tj], live[ti, tj], dense)
        grad_all = lax.dynamic_update_slice(grad_all, part.reshape(nfac, rows, cols), (jnp.int32(0), (ti * rows).astype(jnp.int32), (tj * cols).astype(jnp.int32)))
        return grad_all, dense

    grad_all = jnp.zeros(loadings.shape, jnp.float32)
    dense = jnp.zeros(gene_factors.shape, jnp.float32)
    grad_all, dense = lax.fori_loop(0, tiles_x * tiles_y, per_tile, (grad_all, dense))
    wide = loadings.astype(jnp.float32)
    padded = jnp.pad(wide, ((0, 0), (1, 1), (1, 1)))
    beside = padded[:, 2:, 1:-1] + padded[:, :-2, 1:-1] + padded[:, 1:-1, 2:] + padded[:, 1:-1, :-2]
    laplace = 4.0 * wide - beside
    grad_loadings = grad_all + 0.5 * laplace
    grad_genes = dense / (rows * cols * tiles_x)
    return grad_loadings, grad_genes
```

```python
import functools
import jax
import jax.numpy as jnp
from jax import lax
from jax.experimental import pallas as pl
from jax.experimental.pallas import tpu as pltpu
from jax.sharding import PartitionSpec as P

MESH = pl.DeviceIdType.MESH
GROUP = 4


def extended(value, sides, width):
    for axis, dim in sides:
        devices, length = (lax.axis_size(axis), value.shape[dim])
        up = [(i, (i + 1) % devices) for i in range(devices - 1)]
        down = [(j, i) for i, j in up]
        last = lax.slice_in_dim(value, length - width, length, axis=dim)
        initial = lax.slice_in_dim(value, 0, width, axis=dim)
        before = lax.ppermute(last, axis, up)
        after = lax.ppermute(initial, axis, down)
        value = jnp.concatenate([before, value, after], axis=dim)
    return value


def by_collectives(loadings, gene_factors, counts, block_ids, live):
    nfac = loadings.shape[0]
    rows = loadings.shape[1]
    cols = loadings.shape[2]
    spots = rows * cols
    factors = lax.all_gather(gene_factors, "sy", axis=0, tiled=True)
    wflat = loadings.reshape(nfac, spots)
    tile_counts = counts[0, 0]
    tile_ids = block_ids[0, 0]

    def step(n, carry):
        grad_part, dense_acc = carry
        block = tile_ids[n]
        block_factor = lax.dynamic_index_in_dim(factors, block, 0, keepdims=False)
        block_counts = lax.dynamic_index_in_dim(tile_counts, n, 0, keepdims=False)
        rate = lax.dot_general(
            block_factor, wflat, (((0,), (0,)), ((), ())), preferred_element_type=jnp.float32
        )
        ratio = (1.0 - block_counts.astype(jnp.float32) / rate).astype(jnp.bfloat16)
        grad_part = grad_part + lax.dot_general(
            block_factor, ratio, (((1,), (0,)), ((), ())), preferred_element_type=jnp.float32
        )
        gene_term = lax.dot_general(
            wflat, ratio, (((1,), (1,)), ((), ())), preferred_element_type=jnp.float32
        )
        old = lax.dynamic_index_in_dim(dense_acc, block, 0, keepdims=True)
        dense_acc = lax.dynamic_update_index_in_dim(dense_acc, old + gene_term[None], block, 0)
        return (grad_part, dense_acc)

    start = jnp.zeros((nfac, spots), jnp.float32)
    dense = jnp.zeros(factors.shape, jnp.float32)
    grad_part, dense = lax.fori_loop(0, live[0, 0], step, (start, dense))
    padded = extended(loadings, (("sx", 1), ("sy", 2)), 1).astype(jnp.float32)
    beside = padded[:, 2:, 1:-1] + padded[:, :-2, 1:-1] + padded[:, 1:-1, 2:] + padded[:, 1:-1, :-2]
    laplace = 4.0 * loadings.astype(jnp.float32) - beside
    grad_loadings = grad_part.reshape(nfac, rows, cols) + 0.5 * laplace
    row_count = lax.axis_size("sx")
    slab = lax.psum_scatter(dense, "sy", scatter_dimension=0, tiled=True)
    summed = lax.psum(slab, "sx")
    grad_genes = summed / (spots * row_count)
    return (grad_loadings, grad_genes)


def kernel(nx, ny, rows, ids, inv, live, w, gf, counts, out_l, out_g,
           facs, cbuf, terms, hl, hr, hu, hd, s_a, r_a, s_b, r_b, s_c, r_c, s_d, r_d,
           csem, hs, hrs, g1s, g1r, g2s, g2r, g3s, g3r, g4s, g4r,
           as_, ar, bs, br, cs, cr, ds_, dr):
    i = lax.axis_index("sx")
    j = lax.axis_index("sy")
    x = i // 2
    c = i % 2
    sib = x * 2 + (1 - c)
    opp = (1 - x) * 2 + c
    diag = (1 - x) * 2 + (1 - c)
    own = gf.shape[0]
    q = own // nx
    cols = w.shape[1] // rows
    spots = w.shape[1]
    slots = counts.shape[0]
    genes = counts.shape[1]

    def remote(src, dst, ss, rs, di, dj):
        return pltpu.make_async_remote_copy(
            src_ref=src, dst_ref=dst, send_sem=ss, recv_sem=rs, device_id=(di, dj), device_id_type=MESH
        )

    load = pltpu.make_async_copy(counts, cbuf, csem)
    load.start()

    barrier = pltpu.get_barrier_semaphore()
    for p in (sib, opp, diag):
        pl.semaphore_signal(barrier, inc=1, device_id=(p, j), device_id_type=MESH)
    for d in range(1, ny):
        pl.semaphore_signal(barrier, inc=1, device_id=(i, lax.rem(j + d, ny)), device_id_type=MESH)
    pl.semaphore_wait(barrier, 3 + ny - 1)

    g1, g2, g3, g4 = [], [], [], []
    for d in range(1, ny):
        dst = lax.rem(j + d, ny)
        g1.append(remote(gf.at[pl.ds(q * i, q)], facs.at[pl.ds(j * own + q * i, q)],
                         g1s.at[d - 1], g1r.at[d - 1], i, dst))
        src = lax.rem(j + ny - d, ny)
        mine = facs.at[pl.ds(src * own + q * i, q)]
        other = facs.at[pl.ds(src * own + q * opp, q)]
        g2.append(remote(mine, mine, g2s.at[d - 1], g2r.at[d - 1], opp, j))
        g3.append(remote(mine, mine, g3s.at[d - 1], g3r.at[d - 1], sib, j))
        g4.append(remote(other, other, g4s.at[d - 1], g4r.at[d - 1], sib, j))
    order = sorted(range(ny - 1), key=lambda d: min(d + 1, ny - 1 - d))
    for d in order[::-1]:
        g1[d].start()
    halo = [
        remote(w, hl, hs.at[0], hrs.at[0], i, lax.rem(j + 1, ny)),
        remote(w, hr, hs.at[1], hrs.at[1], i, lax.rem(j + ny - 1, ny)),
        remote(w.at[:, pl.ds((rows - 1) * cols, cols)], hu, hs.at[2], hrs.at[2], lax.rem(i + 1, nx), j),
        remote(w.at[:, pl.ds(0, cols)], hd, hs.at[3], hrs.at[3], lax.rem(i + nx - 1, nx), j),
    ]
    facs[pl.ds(j * own, own)] = gf[...]
    terms[slots] = jnp.zeros(terms.shape[1:], jnp.float32)
    out_l[...] = jnp.zeros_like(out_l)
    for d in order:
        g1[d].wait_recv()
        g2[d].start()
        g3[d].start()
    for h in halo:
        h.start()
    for d in order:
        g2[d].wait_recv()
        g4[d].start()
    for d in order:
        g3[d].wait_recv()
        g4[d].wait_recv()
    load.wait()

    alive = live[0]

    def group(g, _):
        base = g * GROUP
        fs = [facs[ids[base + k]] for k in range(GROUP)]
        f = jnp.concatenate(fs, axis=1)
        wv = w[...]
        rate = lax.dot_general(f, wv, (((0,), (0,)), ((), ())), preferred_element_type=jnp.float32)
        cnt = cbuf[pl.ds(base, GROUP)].reshape(GROUP * genes, spots).astype(jnp.float32)
        inverse = pl.reciprocal(rate, approx=True)
        inverse = inverse * (2.0 - rate * inverse)
        ratio = (1.0 - cnt * inverse).astype(jnp.bfloat16)
        keep = [jnp.where(base + k < alive, 1.0, 0.0).astype(jnp.float32) for k in range(GROUP)]
        fm = jnp.concatenate(
            [(a.astype(jnp.float32) * m).astype(jnp.bfloat16) for a, m in zip(fs, keep)], axis=1
        )
        out_l[...] += lax.dot_general(fm, ratio, (((1,), (0,)), ((), ())), preferred_element_type=jnp.float32)
        term = lax.dot_general(wv, ratio, (((1,), (1,)), ((), ())), preferred_element_type=jnp.float32)
        for k in range(GROUP):
            terms[base + k] = term[:, k * genes:(k + 1) * genes]
        return 0

    lax.fori_loop(0, slots // GROUP, group, 0)

    def owner(t):
        return lax.rem(j + 1 + t, ny)

    def copy_a(t):
        return remote(s_a.at[t], r_a.at[t], as_.at[t], ar.at[t], sib, j)

    def copy_b(t):
        return remote(s_b.at[t], r_b.at[t], bs.at[t], br.at[t], opp, j)

    def copy_c(t):
        return remote(s_c.at[t], r_c.at[t], cs.at[t], cr.at[t], i, owner(t))

    def stage_a(t, _):
        for xq in range(2):
            for k in range(q):
                b = owner(t) * own + q * (xq * 2 + (1 - c)) + k
                s_a[t, xq, k] = terms[inv[b]]
        copy_a(t).start()
        return 0

    def stage_b(t, _):
        copy_a(t).wait_recv()
        for k in range(q):
            b = owner(t) * own + q * opp + k
            s_b[t, k] = terms[inv[b]] + r_a[t, 1 - x, k]
        copy_b(t).start()
        return 0

    def combine(t):
        copy_b(t).wait_recv()
        for k in range(q):
            b = owner(t) * own + q * i + k
            s_c[t, k] = terms[inv[b]] + r_a[t, x, k] + r_b[t, k]

    def stage_c(t, _):
        combine(t)
        copy_c(t).start()
        return 0

    lax.fori_loop(0, ny, stage_a, 0)
    lax.fori_loop(0, ny, stage_b, 0)
    lax.fori_loop(0, ny - 1, stage_c, 0)
    combine(ny - 1)

    for h in halo:
        h.wait()
    lane = lax.broadcasted_iota(jnp.int32, (w.shape[0], cols), 1)
    top = jnp.where(i > 0, 1.0, 0.0).astype(jnp.float32)
    bottom = jnp.where(i < nx - 1, 1.0, 0.0).astype(jnp.float32)
    west = jnp.where(j > 0, 1.0, 0.0).astype(jnp.float32)
    east = jnp.where(j < ny - 1, 1.0, 0.0).astype(jnp.float32)
    parts = [w[:, r * cols:(r + 1) * cols].astype(jnp.float32) for r in range(rows)]
    for r in range(rows):
        cut = slice(r * cols, (r + 1) * cols)
        me = parts[r]
        up = parts[r - 1] if r > 0 else hu[...].astype(jnp.float32) * top
        down = parts[r + 1] if r < rows - 1 else hd[...].astype(jnp.float32) * bottom
        lnb = hl[:, cut].astype(jnp.float32) * west
        rnb = hr[:, cut].astype(jnp.float32) * east
        left = pltpu.roll(jnp.where(lane == cols - 1, lnb, me), 1, 1)
        right = pltpu.roll(jnp.where(lane == 0, rnb, me), cols - 1, 1)
        out_l[:, cut] += 0.5 * (4.0 * me - (down + up + right + left))

    total = s_c[ny - 1]
    for t in range(ny - 1):
        copy_c(t).wait_recv()
        total = total + r_c[t]
    total = total / (spots * nx)
    s_d[...] = total
    peers = (sib, opp, diag)
    share = [remote(s_d, r_d.at[p], ds_.at[p], dr.at[p], peers[p], j) for p in range(3)]
    for p in (1, 2, 0):
        share[p].start()
    out_g[pl.ds(q * i, q)] = total
    for p in range(3):
        share[p].wait_recv()
        out_g[pl.ds(q * peers[p], q)] = r_d[p]
    for p in range(3):
        share[p].wait_send()
    for d in range(ny - 1):
        g1[d].wait_send()
        g2[d].wait_send()
        g3[d].wait_send()
        g4[d].wait_send()

    def drain(t, _):
        copy_a(t).wait_send()
        copy_b(t).wait_send()
        return 0

    def drain_c(t, _):
        copy_c(t).wait_send()
        return 0

    lax.fori_loop(0, ny, drain, 0)
    lax.fori_loop(0, ny - 1, drain_c, 0)


def by_kernel(loadings, gene_factors, counts, block_ids, live):
    nfac, rows, cols = loadings.shape
    spots = rows * cols
    nx, ny = lax.axis_size("sx"), lax.axis_size("sy")
    own, _, genes = gene_factors.shape
    slots = counts.shape[2]
    q = own // nx
    ids = block_ids[0, 0]
    slot = jnp.arange(slots, dtype=jnp.int32)
    hit = (ids[None, :] == jnp.arange(own * ny, dtype=jnp.int32)[:, None]) & (slot < live[0, 0])[None, :]
    inv = jnp.min(jnp.where(hit, slot[None, :], slots), axis=1).astype(jnp.int32)
    dma = pltpu.SemaphoreType.DMA
    f32, bf16 = jnp.float32, jnp.bfloat16
    smem = pl.BlockSpec(memory_space=pltpu.SMEM)
    vmem = pl.BlockSpec(memory_space=pltpu.VMEM)
    grad_l, grad_g = pl.pallas_call(
        functools.partial(kernel, nx, ny, rows),
        out_shape=(
            jax.ShapeDtypeStruct((nfac, spots), f32),
            jax.ShapeDtypeStruct((own, nfac, genes), f32),
        ),
        in_specs=[smem, smem, smem, vmem, vmem, pl.BlockSpec(memory_space=pl.ANY)],
        out_specs=(vmem, vmem),
        scratch_shapes=[
            pltpu.VMEM((ny * own, nfac, genes), bf16),
            pltpu.VMEM((slots, genes, spots), bf16),
            pltpu.VMEM((slots + 1, nfac, genes), f32),
            pltpu.VMEM((nfac, spots), bf16),
            pltpu.VMEM((nfac, spots), bf16),
            pltpu.VMEM((nfac, cols), bf16),
            pltpu.VMEM((nfac, cols), bf16),
            pltpu.VMEM((ny, 2, q, nfac, genes), f32),
            pltpu.VMEM((ny, 2, q, nfac, genes), f32),
            pltpu.VMEM((ny, q, nfac, genes), f32),
            pltpu.VMEM((ny, q, nfac, genes), f32),
            pltpu.VMEM((ny, q, nfac, genes), f32),
            pltpu.VMEM((ny - 1, q, nfac, genes), f32),
            pltpu.VMEM((q, nfac, genes), f32),
            pltpu.VMEM((3, q, nfac, genes), f32),
            dma, dma((4,)), dma((4,)),
        ] + [dma((ny - 1,))] * 8 + [dma((ny,))] * 4 + [dma((ny - 1,))] * 2 + [dma((3,))] * 2,
        compiler_params=pltpu.CompilerParams(
            collective_id=0, has_side_effects=True, vmem_limit_bytes=40 * 1024 * 1024
        ),
    )(ids, inv, live[0], loadings.reshape(nfac, spots), gene_factors, counts[0, 0])
    return grad_l.reshape(nfac, rows, cols), grad_g


def on_device(loadings, gene_factors, counts, block_ids, live):
    nx, ny = lax.axis_size("sx"), lax.axis_size("sy")
    fits = nx == 4 and ny > 1 and gene_factors.shape[0] % nx == 0
    fits = fits and loadings.shape[2] % 128 == 0 and counts.shape[2] % GROUP == 0
    form = by_kernel if fits else by_collectives
    return form(loadings, gene_factors, counts, block_ids, live)


def solution(mesh):
    return jax.shard_map(
        on_device,
        mesh=mesh,
        in_specs=(
            P(None, "sx", "sy"),
            P("sy", None, None),
            P("sx", "sy", None, None, None),
            P("sx", "sy", None),
            P("sx", "sy"),
        ),
        out_specs=(P(None, "sx", "sy"), P("sy", None, None)),
        check_vma=False,
    )
```

```python
import functools
import jax
import jax.numpy as jnp
from jax import lax
from jax.experimental import pallas as pl
from jax.experimental.pallas import tpu as pltpu
from jax.sharding import PartitionSpec as P

MESH = pl.DeviceIdType.MESH
GROUP = 4


def extended(value, sides, width):
    for axis, dim in sides:
        devices, length = (lax.axis_size(axis), value.shape[dim])
        up = [(i, (i + 1) % devices) for i in range(devices - 1)]
        down = [(j, i) for i, j in up]
        last = lax.slice_in_dim(value, length - width, length, axis=dim)
        initial = lax.slice_in_dim(value, 0, width, axis=dim)
        before = lax.ppermute(last, axis, up)
        after = lax.ppermute(initial, axis, down)
        value = jnp.concatenate([before, value, after], axis=dim)
    return value


def by_collectives(loadings, gene_factors, counts, block_ids, live):
    nfac = loadings.shape[0]
    rows = loadings.shape[1]
    cols = loadings.shape[2]
    spots = rows * cols
    factors = lax.all_gather(gene_factors, "sy", axis=0, tiled=True)
    wflat = loadings.reshape(nfac, spots)
    tile_counts = counts[0, 0]
    tile_ids = block_ids[0, 0]

    def step(n, carry):
        grad_part, dense_acc = carry
        block = tile_ids[n]
        block_factor = lax.dynamic_index_in_dim(factors, block, 0, keepdims=False)
        block_counts = lax.dynamic_index_in_dim(tile_counts, n, 0, keepdims=False)
        rate = lax.dot_general(
            block_factor, wflat, (((0,), (0,)), ((), ())), preferred_element_type=jnp.float32
        )
        ratio = (1.0 - block_counts.astype(jnp.float32) / rate).astype(jnp.bfloat16)
        grad_part = grad_part + lax.dot_general(
            block_factor, ratio, (((1,), (0,)), ((), ())), preferred_element_type=jnp.float32
        )
        gene_term = lax.dot_general(
            wflat, ratio, (((1,), (1,)), ((), ())), preferred_element_type=jnp.float32
        )
        old = lax.dynamic_index_in_dim(dense_acc, block, 0, keepdims=True)
        dense_acc = lax.dynamic_update_index_in_dim(dense_acc, old + gene_term[None], block, 0)
        return (grad_part, dense_acc)

    start = jnp.zeros((nfac, spots), jnp.float32)
    dense = jnp.zeros(factors.shape, jnp.float32)
    grad_part, dense = lax.fori_loop(0, live[0, 0], step, (start, dense))
    padded = extended(loadings, (("sx", 1), ("sy", 2)), 1).astype(jnp.float32)
    beside = padded[:, 2:, 1:-1] + padded[:, :-2, 1:-1] + padded[:, 1:-1, 2:] + padded[:, 1:-1, :-2]
    laplace = 4.0 * loadings.astype(jnp.float32) - beside
    grad_loadings = grad_part.reshape(nfac, rows, cols) + 0.5 * laplace
    row_count = lax.axis_size("sx")
    slab = lax.psum_scatter(dense, "sy", scatter_dimension=0, tiled=True)
    summed = lax.psum(slab, "sx")
    grad_genes = summed / (spots * row_count)
    return (grad_loadings, grad_genes)


def kernel(nx, ny, rows, ids, inv, live, w, gf, counts, out_l, out_g,
           facs, cbuf, terms, hl, hr, hu, hd, s_a, r_a, s_b, r_b, s_c, r_c, s_d, r_d, s_e, r_e,
           csem, fsem, hs, hrs, ga, gar, gb, gbr, gc, gcr, gd, gdr,
           as_, ar, bs, br, cs, cr, ds_, dr, es, er):
    i = lax.axis_index("sx")
    j = lax.axis_index("sy")
    x, c = i // 2, i % 2
    z, y = j // 2, j % 2
    sib = x * 2 + (1 - c)
    opp = (1 - x) * 2 + c
    diag = (1 - x) * 2 + (1 - c)
    nz = ny // 2
    own = gf.shape[0]
    q = own // nx
    cols = w.shape[1] // rows
    spots = w.shape[1]
    slots = counts.shape[0]
    genes = counts.shape[1]
    u, v = x * (1 - c) + y * c, y * (1 - c) + x * c
    zs = [lax.rem(z + 2, nz), nz - 1 - z, z + 1 - 2 * (z % 2), z]

    def at(uu, vv):
        return uu * (1 - c) + vv * c, vv * (1 - c) + uu * c

    def remote(src, dst, ss, rs, di, dj):
        return pltpu.make_async_remote_copy(
            src_ref=src, dst_ref=dst, send_sem=ss, recv_sem=rs, device_id=(di, dj), device_id_type=MESH
        )

    def to(src, dst, ss, rs, uu, vv, zz):
        xx, yy = at(uu, vv)
        return remote(src, dst, ss, rs, xx * 2 + c, zz * 2 + yy)

    def first(uu, vv, zz):
        xx, yy = at(uu, vv)
        return (zz * 2 + yy) * own + q * (xx * 2 + c)

    barrier = pltpu.get_barrier_semaphore()
    for p in (sib, opp, diag):
        pl.semaphore_signal(barrier, inc=1, device_id=(p, j), device_id_type=MESH)
    for d in range(1, ny):
        pl.semaphore_signal(barrier, inc=1, device_id=(i, lax.rem(j + d, ny)), device_id_type=MESH)
    mine = pl.ds(j * own + q * i, q)
    fetch = pltpu.make_async_copy(gf.at[pl.ds(q * i, q)], facs.at[mine], fsem)
    fetch.start()
    load = pltpu.make_async_copy(counts, cbuf, csem)
    load.start()
    terms[slots] = jnp.zeros(terms.shape[1:], jnp.float32)
    out_l[...] = jnp.zeros_like(out_l)
    fetch.wait()
    pl.semaphore_wait(barrier, 3 + ny - 1)

    last = nz - 1
    cd, cc, cb, ca = {}, {}, {}, {}
    for t in range(nz):
        p0 = facs.at[pl.ds(first(u, v, zs[t]), q)]
        p1 = facs.at[pl.ds(first(u, 1 - v, zs[t]), q)]
        p2 = facs.at[pl.ds(first(1 - u, v, zs[t]), q)]
        p3 = facs.at[pl.ds(first(1 - u, 1 - v, zs[t]), q)]
        if t < last:
            own_piece = facs.at[mine]
            cd[t] = to(own_piece, own_piece, gd.at[t], gdr.at[t], u, v, zs[t])
        cc[t] = to(p0, p0, gc.at[t], gcr.at[t], u, 1 - v, z)
        cb[t, 1] = to(p0, p0, gb.at[t, 1], gbr.at[t, 0 + 1], 1 - u, v, z)
        cb[t, 0] = to(p1, p1, gb.at[t, 0], gbr.at[t, 0], 1 - u, v, z)
        for e, piece in enumerate((p0, p1, p2, p3)):
            ca[t, e] = remote(piece, piece, ga.at[t, e], gar.at[t, e], sib, j)

    def have(t):
        cb[t, 1].start()
        cc[t].start()
        ca[t, 0].start()

    def got_d(t):
        cd[t].wait_recv()
        have(t)

    def got_c(t):
        cc[t].wait_recv()
        cb[t, 0].start()
        ca[t, 1].start()

    def got_b(t, e):
        cb[t, e].wait_recv()
        ca[t, 3 - e].start()

    for t in range(last):
        cd[t].start()
    have(last)
    got_c(3), got_d(2), got_b(3, 1), got_d(1), got_c(2), got_d(0), got_b(3, 0), got_b(2, 1), got_c(1)
    got_b(2, 0), got_b(1, 1), got_c(0), got_b(1, 0), got_b(0, 1), got_b(0, 0)
    halo = [
        remote(w, hl, hs.at[0], hrs.at[0], i, lax.rem(j + 1, ny)),
        remote(w, hr, hs.at[1], hrs.at[1], i, lax.rem(j + ny - 1, ny)),
        remote(w.at[:, pl.ds((rows - 1) * cols, cols)], hu, hs.at[2], hrs.at[2], lax.rem(i + 1, nx), j),
        remote(w.at[:, pl.ds(0, cols)], hd, hs.at[3], hrs.at[3], lax.rem(i + nx - 1, nx), j),
    ]
    for h in halo:
        h.start()
    for t in range(nz):
        for e in range(4):
            ca[t, e].wait_recv()
    load.wait()

    alive = live[0]

    def group(g, _):
        base = g * GROUP
        fs = [facs[ids[base + k]] for k in range(GROUP)]
        f = jnp.concatenate(fs, axis=1)
        wv = w[...]
        rate = lax.dot_general(f, wv, (((0,), (0,)), ((), ())), preferred_element_type=jnp.float32)
        cnt = cbuf[pl.ds(base, GROUP)].reshape(GROUP * genes, spots).astype(jnp.float32)
        inverse = pl.reciprocal(rate, approx=True)
        inverse = inverse * (2.0 - rate * inverse)
        ratio = (1.0 - cnt * inverse).astype(jnp.bfloat16)
        keep = [jnp.where(base + k < alive, 1.0, 0.0).astype(jnp.float32) for k in range(GROUP)]
        fm = jnp.concatenate(
            [(a.astype(jnp.float32) * m).astype(jnp.bfloat16) for a, m in zip(fs, keep)], axis=1
        )
        out_l[...] += lax.dot_general(fm, ratio, (((1,), (0,)), ((), ())), preferred_element_type=jnp.float32)
        term = lax.dot_general(wv, ratio, (((1,), (1,)), ((), ())), preferred_element_type=jnp.float32)
        for k in range(GROUP):
            terms[base + k] = term[:, k * genes:(k + 1) * genes]
        return 0

    lax.fori_loop(0, slots // GROUP, group, 0)

    a_, b_, c_, d_ = {}, {}, {}, {}
    for t in range(nz):
        a_[t] = remote(s_a.at[t], r_a.at[t], as_.at[t], ar.at[t], sib, j)
        for e in range(2):
            b_[t, e] = to(s_b.at[t, e], r_b.at[t, e], bs.at[t, e], br.at[t, e], 1 - u, v, z)
        c_[t] = to(s_c.at[t], r_c.at[t], cs.at[t], cr.at[t], u, 1 - v, z)
        if t < last:
            d_[t] = to(s_d.at[t], r_d.at[t], ds_.at[t], dr.at[t], u, v, zs[t])

    for t in range(nz):
        for xx in range(2):
            for yy in range(2):
                for k in range(q):
                    b = (zs[t] * 2 + yy) * own + q * (xx * 2 + (1 - c)) + k
                    s_a[t, xx, yy, k] = terms[inv[b]]
        a_[t].start()

    def partial(t, uu, vv, k):
        xx, yy = at(uu, vv)
        return terms[inv[first(uu, vv, zs[t]) + k]] + r_a[t, xx, yy, k]

    for t in range(nz):
        a_[t].wait_recv()
        for e in range(2):
            for k in range(q):
                s_b[t, e, k] = partial(t, 1 - u, v if e else 1 - v, k)
            b_[t, e].start()

    def stage_c(t):
        b_[t, 0].wait_recv()
        for k in range(q):
            s_c[t, k] = partial(t, u, 1 - v, k) + r_b[t, 0, k]
        c_[t].start()

    def stage_d(t):
        b_[t, 1].wait_recv()
        c_[t].wait_recv()
        for k in range(q):
            s_d[t, k] = partial(t, u, v, k) + r_b[t, 1, k] + r_c[t, k]
        if t < last:
            d_[t].start()

    stage_c(0)
    for t in range(1, nz):
        stage_c(t)
        stage_d(t - 1)

    for h in halo:
        h.wait()
    lane = lax.broadcasted_iota(jnp.int32, (w.shape[0], cols), 1)
    top = jnp.where(i > 0, 1.0, 0.0).astype(jnp.float32)
    bottom = jnp.where(i < nx - 1, 1.0, 0.0).astype(jnp.float32)
    west = jnp.where(j > 0, 1.0, 0.0).astype(jnp.float32)
    east = jnp.where(j < ny - 1, 1.0, 0.0).astype(jnp.float32)
    parts = [w[:, r * cols:(r + 1) * cols].astype(jnp.float32) for r in range(rows)]
    for r in range(rows):
        cut = slice(r * cols, (r + 1) * cols)
        me = parts[r]
        up = parts[r - 1] if r > 0 else hu[...].astype(jnp.float32) * top
        down = parts[r + 1] if r < rows - 1 else hd[...].astype(jnp.float32) * bottom
        lnb = hl[:, cut].astype(jnp.float32) * west
        rnb = hr[:, cut].astype(jnp.float32) * east
        left = pltpu.roll(jnp.where(lane == cols - 1, lnb, me), 1, 1)
        right = pltpu.roll(jnp.where(lane == 0, rnb, me), cols - 1, 1)
        out_l[:, cut] += 0.5 * (4.0 * me - (down + up + right + left))

    stage_d(last)
    for t in range(last):
        d_[t].wait_recv()
    near, over, pass_on = [], [], []
    for k in range(q):
        total = s_d[last, k]
        for t in range(last):
            total = total + r_d[t, k]
        total = total / (spots * nx)
        s_e[k] = total
        over.append(remote(s_e.at[k], r_e.at[0, k], es.at[0, k], er.at[0, k], opp, j))
        near.append(remote(s_e.at[k], r_e.at[1, k], es.at[1, k], er.at[1, k], sib, j))
        pass_on.append(remote(r_e.at[0, k], r_e.at[2, k], es.at[2, k], er.at[2, k], sib, j))
        over[k].start()
        near[k].start()
        out_g[q * i + k] = total
    for k in range(q):
        over[k].wait_recv()
        pass_on[k].start()
        out_g[q * opp + k] = r_e[0, k]
    for k in range(q):
        near[k].wait_recv()
        out_g[q * sib + k] = r_e[1, k]
    for k in range(q):
        pass_on[k].wait_recv()
        out_g[q * diag + k] = r_e[2, k]
    for group_of in (cd, cc, cb, ca, a_, b_, c_, d_):
        for copy in group_of.values():
            copy.wait_send()
    for copy in over + near + pass_on:
        copy.wait_send()


def by_kernel(loadings, gene_factors, counts, block_ids, live):
    nfac, rows, cols = loadings.shape
    spots = rows * cols
    nx, ny = lax.axis_size("sx"), lax.axis_size("sy")
    own, _, genes = gene_factors.shape
    slots = counts.shape[2]
    q = own // nx
    nz = ny // 2
    ids = block_ids[0, 0]
    slot = jnp.arange(slots, dtype=jnp.int32)
    hit = (ids[None, :] == jnp.arange(own * ny, dtype=jnp.int32)[:, None]) & (slot < live[0, 0])[None, :]
    inv = jnp.min(jnp.where(hit, slot[None, :], slots), axis=1).astype(jnp.int32)
    dma = pltpu.SemaphoreType.DMA
    f32, bf16 = jnp.float32, jnp.bfloat16
    smem = pl.BlockSpec(memory_space=pltpu.SMEM)
    vmem = pl.BlockSpec(memory_space=pltpu.VMEM)
    grad_l, grad_g = pl.pallas_call(
        functools.partial(kernel, nx, ny, rows),
        out_shape=(
            jax.ShapeDtypeStruct((nfac, spots), f32),
            jax.ShapeDtypeStruct((own, nfac, genes), f32),
        ),
        in_specs=[smem, smem, smem, vmem] + [pl.BlockSpec(memory_space=pl.ANY)] * 2,
        out_specs=(vmem, vmem),
        scratch_shapes=[
            pltpu.VMEM((ny * own, nfac, genes), bf16),
            pltpu.VMEM((slots, genes, spots), bf16),
            pltpu.VMEM((slots + 1, nfac, genes), f32),
            pltpu.VMEM((nfac, spots), bf16),
            pltpu.VMEM((nfac, spots), bf16),
            pltpu.VMEM((nfac, cols), bf16),
            pltpu.VMEM((nfac, cols), bf16),
            pltpu.VMEM((nz, 2, 2, q, nfac, genes), f32),
            pltpu.VMEM((nz, 2, 2, q, nfac, genes), f32),
            pltpu.VMEM((nz, 2, q, nfac, genes), f32),
            pltpu.VMEM((nz, 2, q, nfac, genes), f32),
            pltpu.VMEM((nz, q, nfac, genes), f32),
            pltpu.VMEM((nz, q, nfac, genes), f32),
            pltpu.VMEM((nz, q, nfac, genes), f32),
            pltpu.VMEM((nz - 1, q, nfac, genes), f32),
            pltpu.VMEM((q, nfac, genes), f32),
            pltpu.VMEM((3, q, nfac, genes), f32),
            dma, dma, dma((4,)), dma((4,)),
        ] + [dma((nz, 4))] * 2 + [dma((nz, 2))] * 2 + [dma((nz,))] * 2 + [dma((nz - 1,))] * 2
        + [dma((nz,))] * 2 + [dma((nz, 2))] * 2 + [dma((nz,))] * 2 + [dma((nz - 1,))] * 2
        + [dma((3, q))] * 2,
        compiler_params=pltpu.CompilerParams(
            collective_id=0, has_side_effects=True, vmem_limit_bytes=60 * 1024 * 1024
        ),
    )(ids, inv, live[0], loadings.reshape(nfac, spots), gene_factors, counts[0, 0])
    return grad_l.reshape(nfac, rows, cols), grad_g


def on_device(loadings, gene_factors, counts, block_ids, live):
    nx, ny = lax.axis_size("sx"), lax.axis_size("sy")
    fits = nx == 4 and ny == 8 and gene_factors.shape[0] % nx == 0
    fits = fits and loadings.shape[2] % 128 == 0 and counts.shape[2] % GROUP == 0
    form = by_kernel if fits else by_collectives
    return form(loadings, gene_factors, counts, block_ids, live)


def solution(mesh):
    return jax.shard_map(
        on_device,
        mesh=mesh,
        in_specs=(
            P(None, "sx", "sy"),
            P("sy", None, None),
            P("sx", "sy", None, None, None),
            P("sx", "sy", None),
            P("sx", "sy"),
        ),
        out_specs=(P(None, "sx", "sy"), P("sy", None, None)),
        check_vma=False,
    )
```

```python
import functools
import jax
import jax.numpy as jnp
from jax import lax
from jax.experimental import pallas as pl
from jax.experimental.pallas import tpu as pltpu
from jax.sharding import PartitionSpec as P

MESH = pl.DeviceIdType.MESH
GROUP = 4


def extended(value, sides, width):
    for axis, dim in sides:
        devices, length = (lax.axis_size(axis), value.shape[dim])
        up = [(i, (i + 1) % devices) for i in range(devices - 1)]
        down = [(j, i) for i, j in up]
        last = lax.slice_in_dim(value, length - width, length, axis=dim)
        initial = lax.slice_in_dim(value, 0, width, axis=dim)
        before = lax.ppermute(last, axis, up)
        after = lax.ppermute(initial, axis, down)
        value = jnp.concatenate([before, value, after], axis=dim)
    return value


def by_collectives(loadings, gene_factors, counts, block_ids, live):
    nfac = loadings.shape[0]
    rows = loadings.shape[1]
    cols = loadings.shape[2]
    spots = rows * cols
    factors = lax.all_gather(gene_factors, "sy", axis=0, tiled=True)
    wflat = loadings.reshape(nfac, spots)
    tile_counts = counts[0, 0]
    tile_ids = block_ids[0, 0]

    def step(n, carry):
        grad_part, dense_acc = carry
        block = tile_ids[n]
        block_factor = lax.dynamic_index_in_dim(factors, block, 0, keepdims=False)
        block_counts = lax.dynamic_index_in_dim(tile_counts, n, 0, keepdims=False)
        rate = lax.dot_general(
            block_factor, wflat, (((0,), (0,)), ((), ())), preferred_element_type=jnp.float32
        )
        ratio = (1.0 - block_counts.astype(jnp.float32) / rate).astype(jnp.bfloat16)
        grad_part = grad_part + lax.dot_general(
            block_factor, ratio, (((1,), (0,)), ((), ())), preferred_element_type=jnp.float32
        )
        gene_term = lax.dot_general(
            wflat, ratio, (((1,), (1,)), ((), ())), preferred_element_type=jnp.float32
        )
        old = lax.dynamic_index_in_dim(dense_acc, block, 0, keepdims=True)
        dense_acc = lax.dynamic_update_index_in_dim(dense_acc, old + gene_term[None], block, 0)
        return (grad_part, dense_acc)

    start = jnp.zeros((nfac, spots), jnp.float32)
    dense = jnp.zeros(factors.shape, jnp.float32)
    grad_part, dense = lax.fori_loop(0, live[0, 0], step, (start, dense))
    padded = extended(loadings, (("sx", 1), ("sy", 2)), 1).astype(jnp.float32)
    beside = padded[:, 2:, 1:-1] + padded[:, :-2, 1:-1] + padded[:, 1:-1, 2:] + padded[:, 1:-1, :-2]
    laplace = 4.0 * loadings.astype(jnp.float32) - beside
    grad_loadings = grad_part.reshape(nfac, rows, cols) + 0.5 * laplace
    row_count = lax.axis_size("sx")
    slab = lax.psum_scatter(dense, "sy", scatter_dimension=0, tiled=True)
    summed = lax.psum(slab, "sx")
    grad_genes = summed / (spots * row_count)
    return (grad_loadings, grad_genes)


def encode(dst, values):
    top = functools.reduce(jnp.maximum, [jnp.max(jnp.abs(a), axis=0, keepdims=True) for a in values])
    power = jnp.floor(jnp.log2(jnp.maximum(top, 1e-30))) - 13.0
    factor = jnp.exp2(-power)
    n = values[0].shape[0]
    for k, a in enumerate(values):
        dst[k * n:(k + 1) * n] = jnp.floor(a * factor + 0.5).astype(jnp.int32).astype(jnp.int16)
    tail = jnp.broadcast_to(power.astype(jnp.int32), (16, top.shape[1]))
    dst[len(values) * n:len(values) * n + 16] = tail.astype(jnp.int16)


def decode(src, count, n):
    power = src[count * n:count * n + 16].astype(jnp.int32).astype(jnp.float32)
    factor = jnp.exp2(power[0:1])
    return [src[k * n:(k + 1) * n].astype(jnp.int32).astype(jnp.float32) * factor for k in range(count)]


def kernel(nx, ny, rows, ids, inv, live, w, gf, counts, out_l, out_g,
           facs, cbuf, terms, hl, hr, hu, hd, s_a, r_a, s_b, r_b, s_c, r_c, s_d, r_d, s_e, r_e,
           csem, fsem, hs, hrs, ga, gar, gb, gbr, gc, gcr, gd, gdr,
           as_, ar, bs, br, cs, cr, ds_, dr, es, er):
    i = lax.axis_index("sx")
    j = lax.axis_index("sy")
    x, c = i // 2, i % 2
    z, y = j // 2, j % 2
    sib = x * 2 + (1 - c)
    opp = (1 - x) * 2 + c
    diag = (1 - x) * 2 + (1 - c)
    nz = ny // 2
    own = gf.shape[0]
    q = own // nx
    cols = w.shape[1] // rows
    spots = w.shape[1]
    slots = counts.shape[0]
    genes = counts.shape[1]
    nfac = w.shape[0]
    u, v = x * (1 - c) + y * c, y * (1 - c) + x * c
    zs = [lax.rem(z + 2, nz), nz - 1 - z, z + 1 - 2 * (z % 2), z]

    def at(uu, vv):
        return uu * (1 - c) + vv * c, vv * (1 - c) + uu * c

    def remote(src, dst, ss, rs, di, dj):
        return pltpu.make_async_remote_copy(
            src_ref=src, dst_ref=dst, send_sem=ss, recv_sem=rs, device_id=(di, dj), device_id_type=MESH
        )

    def to(src, dst, ss, rs, uu, vv, zz):
        xx, yy = at(uu, vv)
        return remote(src, dst, ss, rs, xx * 2 + c, zz * 2 + yy)

    def first(uu, vv, zz):
        xx, yy = at(uu, vv)
        return (zz * 2 + yy) * own + q * (xx * 2 + c)

    barrier = pltpu.get_barrier_semaphore()
    for p in (sib, opp, diag):
        pl.semaphore_signal(barrier, inc=1, device_id=(p, j), device_id_type=MESH)
    for d in range(1, ny):
        pl.semaphore_signal(barrier, inc=1, device_id=(i, lax.rem(j + d, ny)), device_id_type=MESH)
    mine = pl.ds(j * own + q * i, q)
    fetch = pltpu.make_async_copy(gf.at[pl.ds(q * i, q)], facs.at[mine], fsem)
    fetch.start()
    load = pltpu.make_async_copy(counts, cbuf, csem)
    load.start()
    terms[slots] = jnp.zeros(terms.shape[1:], jnp.float32)
    out_l[...] = jnp.zeros_like(out_l)
    fetch.wait()
    pl.semaphore_wait(barrier, 3 + ny - 1)

    last = nz - 1
    cd, cc, cb, ca = {}, {}, {}, {}
    for t in range(nz):
        p0 = facs.at[pl.ds(first(u, v, zs[t]), q)]
        p1 = facs.at[pl.ds(first(u, 1 - v, zs[t]), q)]
        p2 = facs.at[pl.ds(first(1 - u, v, zs[t]), q)]
        p3 = facs.at[pl.ds(first(1 - u, 1 - v, zs[t]), q)]
        if t < last:
            own_piece = facs.at[mine]
            cd[t] = to(own_piece, own_piece, gd.at[t], gdr.at[t], u, v, zs[t])
        cc[t] = to(p0, p0, gc.at[t], gcr.at[t], u, 1 - v, z)
        cb[t, 1] = to(p0, p0, gb.at[t, 1], gbr.at[t, 0 + 1], 1 - u, v, z)
        cb[t, 0] = to(p1, p1, gb.at[t, 0], gbr.at[t, 0], 1 - u, v, z)
        for e, piece in enumerate((p0, p1, p2, p3)):
            ca[t, e] = remote(piece, piece, ga.at[t, e], gar.at[t, e], sib, j)

    def have(t):
        cb[t, 1].start()
        cc[t].start()
        ca[t, 0].start()

    def got_d(t):
        cd[t].wait_recv()
        have(t)

    def got_c(t):
        cc[t].wait_recv()
        cb[t, 0].start()
        ca[t, 1].start()

    def got_b(t, e):
        cb[t, e].wait_recv()
        ca[t, 3 - e].start()

    for t in range(last):
        cd[t].start()
    have(last)
    got_c(3), got_d(2), got_b(3, 1), got_d(1), got_c(2), got_d(0), got_b(3, 0), got_b(2, 1), got_c(1)
    got_b(2, 0), got_b(1, 1), got_c(0), got_b(1, 0), got_b(0, 1), got_b(0, 0)
    halo = [
        remote(w, hl, hs.at[0], hrs.at[0], i, lax.rem(j + 1, ny)),
        remote(w, hr, hs.at[1], hrs.at[1], i, lax.rem(j + ny - 1, ny)),
        remote(w.at[:, pl.ds((rows - 1) * cols, cols)], hu, hs.at[2], hrs.at[2], lax.rem(i + 1, nx), j),
        remote(w.at[:, pl.ds(0, cols)], hd, hs.at[3], hrs.at[3], lax.rem(i + nx - 1, nx), j),
    ]
    for h in halo:
        h.start()
    for t in range(nz):
        for e in range(4):
            ca[t, e].wait_recv()
    load.wait()

    alive = live[0]

    def group(g, _):
        base = g * GROUP
        fs = [facs[ids[base + k]] for k in range(GROUP)]
        f = jnp.concatenate(fs, axis=1)
        wv = w[...]
        rate = lax.dot_general(f, wv, (((0,), (0,)), ((), ())), preferred_element_type=jnp.float32)
        cnt = cbuf[pl.ds(base, GROUP)].reshape(GROUP * genes, spots).astype(jnp.float32)
        inverse = pl.reciprocal(rate, approx=True)
        inverse = inverse * (2.0 - rate * inverse)
        ratio = (1.0 - cnt * inverse).astype(jnp.bfloat16)
        keep = [jnp.where(base + k < alive, 1.0, 0.0).astype(jnp.float32) for k in range(GROUP)]
        fm = jnp.concatenate(
            [(a.astype(jnp.float32) * m).astype(jnp.bfloat16) for a, m in zip(fs, keep)], axis=1
        )
        out_l[...] += lax.dot_general(fm, ratio, (((1,), (0,)), ((), ())), preferred_element_type=jnp.float32)
        term = lax.dot_general(wv, ratio, (((1,), (1,)), ((), ())), preferred_element_type=jnp.float32)
        for k in range(GROUP):
            terms[base + k] = term[:, k * genes:(k + 1) * genes]
        return 0

    lax.fori_loop(0, slots // GROUP, group, 0)

    a_, b_, c_, d_ = {}, {}, {}, {}
    for t in range(nz):
        a_[t] = remote(s_a.at[t], r_a.at[t], as_.at[t], ar.at[t], sib, j)
        for e in range(2):
            b_[t, e] = to(s_b.at[t, e], r_b.at[t, e], bs.at[t, e], br.at[t, e], 1 - u, v, z)
        c_[t] = to(s_c.at[t], r_c.at[t], cs.at[t], cr.at[t], u, 1 - v, z)
        if t < last:
            d_[t] = to(s_d.at[t], r_d.at[t], ds_.at[t], dr.at[t], u, v, zs[t])

    for t in range(nz):
        for xx in range(2):
            for yy in range(2):
                for k in range(q):
                    b = (zs[t] * 2 + yy) * own + q * (xx * 2 + (1 - c)) + k
                    s_a[t, xx, yy, k] = terms[inv[b]]
        a_[t].start()

    def partial(t, uu, vv, k):
        xx, yy = at(uu, vv)
        return terms[inv[first(uu, vv, zs[t]) + k]] + r_a[t, xx, yy, k]

    for t in range(nz):
        a_[t].wait_recv()
        for e in range(2):
            encode(s_b.at[t, e], [partial(t, 1 - u, v if e else 1 - v, k) for k in range(q)])
            b_[t, e].start()

    def stage_c(t):
        b_[t, 0].wait_recv()
        came = decode(r_b.at[t, 0], q, nfac)
        encode(s_c.at[t], [partial(t, u, 1 - v, k) + came[k] for k in range(q)])
        c_[t].start()

    def stage_d(t):
        b_[t, 1].wait_recv()
        c_[t].wait_recv()
        came, more = decode(r_b.at[t, 1], q, nfac), decode(r_c.at[t], q, nfac)
        for k in range(q):
            s_d[t, k] = partial(t, u, v, k) + came[k] + more[k]
        if t < last:
            d_[t].start()

    stage_c(0)
    for t in range(1, nz):
        stage_c(t)
        stage_d(t - 1)

    for h in halo:
        h.wait()
    lane = lax.broadcasted_iota(jnp.int32, (w.shape[0], cols), 1)
    top = jnp.where(i > 0, 1.0, 0.0).astype(jnp.float32)
    bottom = jnp.where(i < nx - 1, 1.0, 0.0).astype(jnp.float32)
    west = jnp.where(j > 0, 1.0, 0.0).astype(jnp.float32)
    east = jnp.where(j < ny - 1, 1.0, 0.0).astype(jnp.float32)
    parts = [w[:, r * cols:(r + 1) * cols].astype(jnp.float32) for r in range(rows)]
    for r in range(rows):
        cut = slice(r * cols, (r + 1) * cols)
        me = parts[r]
        up = parts[r - 1] if r > 0 else hu[...].astype(jnp.float32) * top
        down = parts[r + 1] if r < rows - 1 else hd[...].astype(jnp.float32) * bottom
        lnb = hl[:, cut].astype(jnp.float32) * west
        rnb = hr[:, cut].astype(jnp.float32) * east
        left = pltpu.roll(jnp.where(lane == cols - 1, lnb, me), 1, 1)
        right = pltpu.roll(jnp.where(lane == 0, rnb, me), cols - 1, 1)
        out_l[:, cut] += 0.5 * (4.0 * me - (down + up + right + left))

    stage_d(last)
    for t in range(last):
        d_[t].wait_recv()
    near, over, pass_on = [], [], []
    for k in range(q):
        total = s_d[last, k]
        for t in range(last):
            total = total + r_d[t, k]
        total = total / (spots * nx)
        s_e[k] = total
        over.append(remote(s_e.at[k], r_e.at[0, k], es.at[0, k], er.at[0, k], opp, j))
        near.append(remote(s_e.at[k], r_e.at[1, k], es.at[1, k], er.at[1, k], sib, j))
        pass_on.append(remote(r_e.at[0, k], r_e.at[2, k], es.at[2, k], er.at[2, k], sib, j))
        over[k].start()
        near[k].start()
        out_g[q * i + k] = total
    for k in range(q):
        over[k].wait_recv()
        pass_on[k].start()
        out_g[q * opp + k] = r_e[0, k]
    for k in range(q):
        near[k].wait_recv()
        out_g[q * sib + k] = r_e[1, k]
    for k in range(q):
        pass_on[k].wait_recv()
        out_g[q * diag + k] = r_e[2, k]
    for group_of in (cd, cc, cb, ca, a_, b_, c_, d_):
        for copy in group_of.values():
            copy.wait_send()
    for copy in over + near + pass_on:
        copy.wait_send()


def by_kernel(loadings, gene_factors, counts, block_ids, live):
    nfac, rows, cols = loadings.shape
    spots = rows * cols
    nx, ny = lax.axis_size("sx"), lax.axis_size("sy")
    own, _, genes = gene_factors.shape
    slots = counts.shape[2]
    q = own // nx
    nz = ny // 2
    ids = block_ids[0, 0]
    slot = jnp.arange(slots, dtype=jnp.int32)
    hit = (ids[None, :] == jnp.arange(own * ny, dtype=jnp.int32)[:, None]) & (slot < live[0, 0])[None, :]
    inv = jnp.min(jnp.where(hit, slot[None, :], slots), axis=1).astype(jnp.int32)
    dma = pltpu.SemaphoreType.DMA
    f32, bf16 = jnp.float32, jnp.bfloat16
    smem = pl.BlockSpec(memory_space=pltpu.SMEM)
    vmem = pl.BlockSpec(memory_space=pltpu.VMEM)
    grad_l, grad_g = pl.pallas_call(
        functools.partial(kernel, nx, ny, rows),
        out_shape=(
            jax.ShapeDtypeStruct((nfac, spots), f32),
            jax.ShapeDtypeStruct((own, nfac, genes), f32),
        ),
        in_specs=[smem, smem, smem, vmem] + [pl.BlockSpec(memory_space=pl.ANY)] * 2,
        out_specs=(vmem, vmem),
        scratch_shapes=[
            pltpu.VMEM((ny * own, nfac, genes), bf16),
            pltpu.VMEM((slots, genes, spots), bf16),
            pltpu.VMEM((slots + 1, nfac, genes), f32),
            pltpu.VMEM((nfac, spots), bf16),
            pltpu.VMEM((nfac, spots), bf16),
            pltpu.VMEM((nfac, cols), bf16),
            pltpu.VMEM((nfac, cols), bf16),
            pltpu.VMEM((nz, 2, 2, q, nfac, genes), f32),
            pltpu.VMEM((nz, 2, 2, q, nfac, genes), f32),
            pltpu.VMEM((nz, 2, q * nfac + 16, genes), jnp.int16),
            pltpu.VMEM((nz, 2, q * nfac + 16, genes), jnp.int16),
            pltpu.VMEM((nz, q * nfac + 16, genes), jnp.int16),
            pltpu.VMEM((nz, q * nfac + 16, genes), jnp.int16),
            pltpu.VMEM((nz, q, nfac, genes), f32),
            pltpu.VMEM((nz - 1, q, nfac, genes), f32),
            pltpu.VMEM((q, nfac, genes), f32),
            pltpu.VMEM((3, q, nfac, genes), f32),
            dma, dma, dma((4,)), dma((4,)),
        ] + [dma((nz, 4))] * 2 + [dma((nz, 2))] * 2 + [dma((nz,))] * 2 + [dma((nz - 1,))] * 2
        + [dma((nz,))] * 2 + [dma((nz, 2))] * 2 + [dma((nz,))] * 2 + [dma((nz - 1,))] * 2
        + [dma((3, q))] * 2,
        compiler_params=pltpu.CompilerParams(
            collective_id=0, has_side_effects=True, vmem_limit_bytes=60 * 1024 * 1024
        ),
    )(ids, inv, live[0], loadings.reshape(nfac, spots), gene_factors, counts[0, 0])
    return grad_l.reshape(nfac, rows, cols), grad_g


def on_device(loadings, gene_factors, counts, block_ids, live):
    nx, ny = lax.axis_size("sx"), lax.axis_size("sy")
    fits = nx == 4 and ny == 8 and gene_factors.shape[0] % nx == 0
    fits = fits and loadings.shape[2] % 128 == 0 and counts.shape[2] % GROUP == 0
    form = by_kernel if fits else by_collectives
    return form(loadings, gene_factors, counts, block_ids, live)


def solution(mesh):
    return jax.shard_map(
        on_device,
        mesh=mesh,
        in_specs=(
            P(None, "sx", "sy"),
            P("sy", None, None),
            P("sx", "sy", None, None, None),
            P("sx", "sy", None),
            P("sx", "sy"),
        ),
        out_specs=(P(None, "sx", "sy"), P("sy", None, None)),
        check_vma=False,
    )
```

```python
import functools
import jax
import jax.numpy as jnp
from jax import lax
from jax.experimental import pallas as pl
from jax.experimental.pallas import tpu as pltpu
from jax.sharding import PartitionSpec as P

MESH = pl.DeviceIdType.MESH
GROUP = 16


def extended(value, sides, width):
    for axis, dim in sides:
        devices, length = (lax.axis_size(axis), value.shape[dim])
        up = [(i, (i + 1) % devices) for i in range(devices - 1)]
        down = [(j, i) for i, j in up]
        last = lax.slice_in_dim(value, length - width, length, axis=dim)
        initial = lax.slice_in_dim(value, 0, width, axis=dim)
        before = lax.ppermute(last, axis, up)
        after = lax.ppermute(initial, axis, down)
        value = jnp.concatenate([before, value, after], axis=dim)
    return value


def by_collectives(loadings, gene_factors, counts, block_ids, live):
    nfac = loadings.shape[0]
    rows = loadings.shape[1]
    cols = loadings.shape[2]
    spots = rows * cols
    factors = lax.all_gather(gene_factors, "sy", axis=0, tiled=True)
    wflat = loadings.reshape(nfac, spots)
    tile_counts = counts[0, 0]
    tile_ids = block_ids[0, 0]

    def step(n, carry):
        grad_part, dense_acc = carry
        block = tile_ids[n]
        block_factor = lax.dynamic_index_in_dim(factors, block, 0, keepdims=False)
        block_counts = lax.dynamic_index_in_dim(tile_counts, n, 0, keepdims=False)
        rate = lax.dot_general(
            block_factor, wflat, (((0,), (0,)), ((), ())), preferred_element_type=jnp.float32
        )
        ratio = (1.0 - block_counts.astype(jnp.float32) / rate).astype(jnp.bfloat16)
        grad_part = grad_part + lax.dot_general(
            block_factor, ratio, (((1,), (0,)), ((), ())), preferred_element_type=jnp.float32
        )
        gene_term = lax.dot_general(
            wflat, ratio, (((1,), (1,)), ((), ())), preferred_element_type=jnp.float32
        )
        old = lax.dynamic_index_in_dim(dense_acc, block, 0, keepdims=True)
        dense_acc = lax.dynamic_update_index_in_dim(dense_acc, old + gene_term[None], block, 0)
        return (grad_part, dense_acc)

    start = jnp.zeros((nfac, spots), jnp.float32)
    dense = jnp.zeros(factors.shape, jnp.float32)
    grad_part, dense = lax.fori_loop(0, live[0, 0], step, (start, dense))
    padded = extended(loadings, (("sx", 1), ("sy", 2)), 1).astype(jnp.float32)
    beside = padded[:, 2:, 1:-1] + padded[:, :-2, 1:-1] + padded[:, 1:-1, 2:] + padded[:, 1:-1, :-2]
    laplace = 4.0 * loadings.astype(jnp.float32) - beside
    grad_loadings = grad_part.reshape(nfac, rows, cols) + 0.5 * laplace
    row_count = lax.axis_size("sx")
    slab = lax.psum_scatter(dense, "sy", scatter_dimension=0, tiled=True)
    summed = lax.psum(slab, "sx")
    grad_genes = summed / (spots * row_count)
    return (grad_loadings, grad_genes)


def encode(dst, values):
    top = functools.reduce(jnp.maximum, [jnp.max(jnp.abs(a), axis=0, keepdims=True) for a in values])
    power = jnp.floor(jnp.log2(jnp.maximum(top, 1e-30))) - 13.0
    factor = jnp.exp2(-power)
    n = values[0].shape[0]
    for k, a in enumerate(values):
        dst[k * n:(k + 1) * n] = jnp.floor(a * factor + 0.5).astype(jnp.int32).astype(jnp.int16)
    tail = jnp.broadcast_to(power.astype(jnp.int32), (16, top.shape[1]))
    dst[len(values) * n:len(values) * n + 16] = tail.astype(jnp.int16)


def decode(src, count, n):
    power = src[count * n:count * n + 16].astype(jnp.int32).astype(jnp.float32)
    factor = jnp.exp2(power[0:1])
    return [src[k * n:(k + 1) * n].astype(jnp.int32).astype(jnp.float32) * factor for k in range(count)]


def kernel(nx, ny, rows, ids, inv, live, w, gf, counts, out_l, out_g,
           facs, cbuf, terms, hl, hr, hu, hd, s_a, r_a, s_b, r_b, s_c, r_c, s_d, r_d, s_e, r_e,
           csem, fsem, hs, hrs, ga, gar, gb, gbr, gc, gcr, gd, gdr,
           as_, ar, bs, br, cs, cr, ds_, dr, es, er):
    i = lax.axis_index("sx")
    j = lax.axis_index("sy")
    x, c = i // 2, i % 2
    z, y = j // 2, j % 2
    sib = x * 2 + (1 - c)
    opp = (1 - x) * 2 + c
    diag = (1 - x) * 2 + (1 - c)
    nz = ny // 2
    own = gf.shape[0]
    q = own // nx
    cols = w.shape[1] // rows
    spots = w.shape[1]
    slots = counts.shape[0]
    genes = counts.shape[1]
    nfac = w.shape[0]
    u, v = x * (1 - c) + y * c, y * (1 - c) + x * c
    zs = [lax.rem(z + 2, nz), nz - 1 - z, z + 1 - 2 * (z % 2), z]

    def at(uu, vv):
        return uu * (1 - c) + vv * c, vv * (1 - c) + uu * c

    def remote(src, dst, ss, rs, di, dj):
        return pltpu.make_async_remote_copy(
            src_ref=src, dst_ref=dst, send_sem=ss, recv_sem=rs, device_id=(di, dj), device_id_type=MESH
        )

    def to(src, dst, ss, rs, uu, vv, zz):
        xx, yy = at(uu, vv)
        return remote(src, dst, ss, rs, xx * 2 + c, zz * 2 + yy)

    def first(uu, vv, zz):
        xx, yy = at(uu, vv)
        return (zz * 2 + yy) * own + q * (xx * 2 + c)

    barrier = pltpu.get_barrier_semaphore()
    for p in (sib, opp, diag):
        pl.semaphore_signal(barrier, inc=1, device_id=(p, j), device_id_type=MESH)
    for d in range(1, ny):
        pl.semaphore_signal(barrier, inc=1, device_id=(i, lax.rem(j + d, ny)), device_id_type=MESH)
    mine = pl.ds(j * own + q * i, q)
    fetch = pltpu.make_async_copy(gf.at[pl.ds(q * i, q)], facs.at[mine], fsem)
    fetch.start()
    load = pltpu.make_async_copy(counts, cbuf, csem)
    load.start()
    terms[slots] = jnp.zeros(terms.shape[1:], jnp.float32)
    out_l[...] = jnp.zeros_like(out_l)
    fetch.wait()
    pl.semaphore_wait(barrier, 3 + ny - 1)

    last = nz - 1
    cd, cc, cb, ca = {}, {}, {}, {}
    for t in range(nz):
        p0 = facs.at[pl.ds(first(u, v, zs[t]), q)]
        p1 = facs.at[pl.ds(first(u, 1 - v, zs[t]), q)]
        p2 = facs.at[pl.ds(first(1 - u, v, zs[t]), q)]
        p3 = facs.at[pl.ds(first(1 - u, 1 - v, zs[t]), q)]
        if t < last:
            own_piece = facs.at[mine]
            cd[t] = to(own_piece, own_piece, gd.at[t], gdr.at[t], u, v, zs[t])
        cc[t] = to(p0, p0, gc.at[t], gcr.at[t], u, 1 - v, z)
        cb[t, 1] = to(p0, p0, gb.at[t, 1], gbr.at[t, 0 + 1], 1 - u, v, z)
        cb[t, 0] = to(p1, p1, gb.at[t, 0], gbr.at[t, 0], 1 - u, v, z)
        for e, piece in enumerate((p0, p1, p2, p3)):
            ca[t, e] = remote(piece, piece, ga.at[t, e], gar.at[t, e], sib, j)

    def have(t):
        cb[t, 1].start()
        cc[t].start()
        ca[t, 0].start()

    def got_d(t):
        cd[t].wait_recv()
        have(t)

    def got_c(t):
        cc[t].wait_recv()
        cb[t, 0].start()
        ca[t, 1].start()

    def got_b(t, e):
        cb[t, e].wait_recv()
        ca[t, 3 - e].start()

    for t in range(last):
        cd[t].start()
    have(last)
    got_c(3), got_d(2), got_b(3, 1), got_d(1), got_c(2), got_d(0), got_b(3, 0), got_b(2, 1), got_c(1)
    got_b(2, 0), got_b(1, 1), got_c(0), got_b(1, 0), got_b(0, 1), got_b(0, 0)
    halo = [
        remote(w, hl, hs.at[0], hrs.at[0], i, lax.rem(j + 1, ny)),
        remote(w, hr, hs.at[1], hrs.at[1], i, lax.rem(j + ny - 1, ny)),
        remote(w.at[:, pl.ds((rows - 1) * cols, cols)], hu, hs.at[2], hrs.at[2], lax.rem(i + 1, nx), j),
        remote(w.at[:, pl.ds(0, cols)], hd, hs.at[3], hrs.at[3], lax.rem(i + nx - 1, nx), j),
    ]
    for h in halo:
        h.start()
    for t in range(nz):
        for e in range(4):
            ca[t, e].wait_recv()
    load.wait()

    alive = live[0]

    def group(g, _):
        base = g * GROUP
        fs = [facs[ids[base + k]] for k in range(GROUP)]
        f = jnp.concatenate(fs, axis=1)
        wv = w[...]
        rate = lax.dot_general(f, wv, (((0,), (0,)), ((), ())), preferred_element_type=jnp.float32)
        cnt = cbuf[pl.ds(base, GROUP)].reshape(GROUP * genes, spots).astype(jnp.float32)
        inverse = pl.reciprocal(rate, approx=True)
        inverse = inverse * (2.0 - rate * inverse)
        ratio = (1.0 - cnt * inverse).astype(jnp.bfloat16)
        keep = [jnp.where(base + k < alive, 1.0, 0.0).astype(jnp.float32) for k in range(GROUP)]
        fm = jnp.concatenate(
            [(a.astype(jnp.float32) * m).astype(jnp.bfloat16) for a, m in zip(fs, keep)], axis=1
        )
        out_l[...] += lax.dot_general(fm, ratio, (((1,), (0,)), ((), ())), preferred_element_type=jnp.float32)
        term = lax.dot_general(wv, ratio, (((1,), (1,)), ((), ())), preferred_element_type=jnp.float32)
        for k in range(GROUP):
            terms[base + k] = term[:, k * genes:(k + 1) * genes]
        return 0

    lax.fori_loop(0, slots // GROUP, group, 0)

    a_, b_, c_, d_ = {}, {}, {}, {}
    for t in range(nz):
        a_[t] = remote(s_a.at[t], r_a.at[t], as_.at[t], ar.at[t], sib, j)
        for e in range(2):
            b_[t, e] = to(s_b.at[t, e], r_b.at[t, e], bs.at[t, e], br.at[t, e], 1 - u, v, z)
        c_[t] = to(s_c.at[t], r_c.at[t], cs.at[t], cr.at[t], u, 1 - v, z)
        if t < last:
            d_[t] = to(s_d.at[t], r_d.at[t], ds_.at[t], dr.at[t], u, v, zs[t])

    for t in range(nz):
        for xx in range(2):
            for yy in range(2):
                for k in range(q):
                    b = (zs[t] * 2 + yy) * own + q * (xx * 2 + (1 - c)) + k
                    s_a[t, xx, yy, k] = terms[inv[b]]
        a_[t].start()

    def partial(t, uu, vv, k):
        xx, yy = at(uu, vv)
        return terms[inv[first(uu, vv, zs[t]) + k]] + r_a[t, xx, yy, k]

    for e in range(2):
        for t in range(nz):
            if e == 0:
                a_[t].wait_recv()
            encode(s_b.at[t, e], [partial(t, 1 - u, v if e else 1 - v, k) for k in range(q)])
            b_[t, e].start()

    def stage_c(t):
        b_[t, 0].wait_recv()
        came = decode(r_b.at[t, 0], q, nfac)
        encode(s_c.at[t], [partial(t, u, 1 - v, k) + came[k] for k in range(q)])
        c_[t].start()

    def stage_d(t):
        b_[t, 1].wait_recv()
        c_[t].wait_recv()
        came, more = decode(r_b.at[t, 1], q, nfac), decode(r_c.at[t], q, nfac)
        sums = [partial(t, u, v, k) + came[k] + more[k] for k in range(q)]
        if t < last:
            encode(s_d.at[t], sums)
            d_[t].start()
        else:
            for k in range(q):
                s_e[k] = sums[k]

    for t in range(nz):
        stage_c(t)
    for t in range(last):
        stage_d(t)

    for h in halo:
        h.wait()
    lane = lax.broadcasted_iota(jnp.int32, (w.shape[0], cols), 1)
    top = jnp.where(i > 0, 1.0, 0.0).astype(jnp.float32)
    bottom = jnp.where(i < nx - 1, 1.0, 0.0).astype(jnp.float32)
    west = jnp.where(j > 0, 1.0, 0.0).astype(jnp.float32)
    east = jnp.where(j < ny - 1, 1.0, 0.0).astype(jnp.float32)
    parts = [w[:, r * cols:(r + 1) * cols].astype(jnp.float32) for r in range(rows)]
    for r in range(rows):
        cut = slice(r * cols, (r + 1) * cols)
        me = parts[r]
        up = parts[r - 1] if r > 0 else hu[...].astype(jnp.float32) * top
        down = parts[r + 1] if r < rows - 1 else hd[...].astype(jnp.float32) * bottom
        lnb = hl[:, cut].astype(jnp.float32) * west
        rnb = hr[:, cut].astype(jnp.float32) * east
        left = pltpu.roll(jnp.where(lane == cols - 1, lnb, me), 1, 1)
        right = pltpu.roll(jnp.where(lane == 0, rnb, me), cols - 1, 1)
        out_l[:, cut] += 0.5 * (4.0 * me - (down + up + right + left))

    stage_d(last)
    for t in range(last):
        d_[t].wait_recv()
    near, over, pass_on = [], [], []
    landed = [decode(r_d.at[t], q, nfac) for t in range(last)]
    for k in range(q):
        total = s_e[k]
        for t in range(last):
            total = total + landed[t][k]
        total = total / (spots * nx)
        s_e[k] = total
        over.append(remote(s_e.at[k], r_e.at[0, k], es.at[0, k], er.at[0, k], opp, j))
        near.append(remote(s_e.at[k], r_e.at[1, k], es.at[1, k], er.at[1, k], sib, j))
        pass_on.append(remote(r_e.at[0, k], r_e.at[2, k], es.at[2, k], er.at[2, k], sib, j))
        over[k].start()
        near[k].start()
        out_g[q * i + k] = total
    for k in range(q):
        over[k].wait_recv()
        pass_on[k].start()
        out_g[q * opp + k] = r_e[0, k]
    for k in range(q):
        near[k].wait_recv()
        out_g[q * sib + k] = r_e[1, k]
    for k in range(q):
        pass_on[k].wait_recv()
        out_g[q * diag + k] = r_e[2, k]
    for group_of in (cd, cc, cb, ca, a_, b_, c_, d_):
        for copy in group_of.values():
            copy.wait_send()
    for copy in over + near + pass_on:
        copy.wait_send()


def by_kernel(loadings, gene_factors, counts, block_ids, live):
    nfac, rows, cols = loadings.shape
    spots = rows * cols
    nx, ny = lax.axis_size("sx"), lax.axis_size("sy")
    own, _, genes = gene_factors.shape
    slots = counts.shape[2]
    q = own // nx
    nz = ny // 2
    ids = block_ids[0, 0]
    slot = jnp.arange(slots, dtype=jnp.int32)
    hit = (ids[None, :] == jnp.arange(own * ny, dtype=jnp.int32)[:, None]) & (slot < live[0, 0])[None, :]
    inv = jnp.min(jnp.where(hit, slot[None, :], slots), axis=1).astype(jnp.int32)
    dma = pltpu.SemaphoreType.DMA
    f32, bf16 = jnp.float32, jnp.bfloat16
    smem = pl.BlockSpec(memory_space=pltpu.SMEM)
    vmem = pl.BlockSpec(memory_space=pltpu.VMEM)
    grad_l, grad_g = pl.pallas_call(
        functools.partial(kernel, nx, ny, rows),
        out_shape=(
            jax.ShapeDtypeStruct((nfac, spots), f32),
            jax.ShapeDtypeStruct((own, nfac, genes), f32),
        ),
        in_specs=[smem, smem, smem, vmem] + [pl.BlockSpec(memory_space=pl.ANY)] * 2,
        out_specs=(vmem, vmem),
        scratch_shapes=[
            pltpu.VMEM((ny * own, nfac, genes), bf16),
            pltpu.VMEM((slots, genes, spots), bf16),
            pltpu.VMEM((slots + 1, nfac, genes), f32),
            pltpu.VMEM((nfac, spots), bf16),
            pltpu.VMEM((nfac, spots), bf16),
            pltpu.VMEM((nfac, cols), bf16),
            pltpu.VMEM((nfac, cols), bf16),
            pltpu.VMEM((nz, 2, 2, q, nfac, genes), f32),
            pltpu.VMEM((nz, 2, 2, q, nfac, genes), f32),
            pltpu.VMEM((nz, 2, q * nfac + 16, genes), jnp.int16),
            pltpu.VMEM((nz, 2, q * nfac + 16, genes), jnp.int16),
            pltpu.VMEM((nz, q * nfac + 16, genes), jnp.int16),
            pltpu.VMEM((nz, q * nfac + 16, genes), jnp.int16),
            pltpu.VMEM((nz - 1, q * nfac + 16, genes), jnp.int16),
            pltpu.VMEM((nz - 1, q * nfac + 16, genes), jnp.int16),
            pltpu.VMEM((q, nfac, genes), f32),
            pltpu.VMEM((3, q, nfac, genes), f32),
            dma, dma, dma((4,)), dma((4,)),
        ] + [dma((nz, 4))] * 2 + [dma((nz, 2))] * 2 + [dma((nz,))] * 2 + [dma((nz - 1,))] * 2
        + [dma((nz,))] * 2 + [dma((nz, 2))] * 2 + [dma((nz,))] * 2 + [dma((nz - 1,))] * 2
        + [dma((3, q))] * 2,
        compiler_params=pltpu.CompilerParams(
            collective_id=0, has_side_effects=True, vmem_limit_bytes=50 * 1024 * 1024
        ),
    )(ids, inv, live[0], loadings.reshape(nfac, spots), gene_factors, counts[0, 0])
    return grad_l.reshape(nfac, rows, cols), grad_g


def on_device(loadings, gene_factors, counts, block_ids, live):
    nx, ny = lax.axis_size("sx"), lax.axis_size("sy")
    fits = nx == 4 and ny == 8 and gene_factors.shape[0] % nx == 0
    fits = fits and loadings.shape[2] % 128 == 0 and counts.shape[2] % GROUP == 0
    form = by_kernel if fits else by_collectives
    return form(loadings, gene_factors, counts, block_ids, live)


def solution(mesh):
    return jax.shard_map(
        on_device,
        mesh=mesh,
        in_specs=(
            P(None, "sx", "sy"),
            P("sy", None, None),
            P("sx", "sy", None, None, None),
            P("sx", "sy", None),
            P("sx", "sy"),
        ),
        out_specs=(P(None, "sx", "sy"), P("sy", None, None)),
        check_vma=False,
    )
```
